32 devices in a mesh: groups: 2 (over x), dp: 2 (over core), tensor: 8 (over z, y).
Axes of the slice: x: 2, y: 2, z: 4, core: 2. Of those that a mesh axis runs over, the one named last changes fastest.
Arguments:
- tokens: bfloat16 [256, 8192], P(('groups', 'dp', 'tensor')), parts along dimension 0, may hold values from -6 to 6
- norm_gain: float32 [8192], replicated, may hold values from 0.25 to 1.75
- gate_weight: bfloat16 [8192, 14336], P(None, ('dp', 'tensor')), may hold values from -0.0625 to 0.0625
- up_weight: bfloat16 [8192, 14336], P(None, ('dp', 'tensor')), may hold values from -0.0625 to 0.0625
- down_weight: bfloat16 [14336, 8192], P(('dp', 'tensor')), may hold values from -0.046875 to 0.046875
Outputs:
- layer_out: bfloat16 [256, 8192], P(('groups', 'dp', 'tensor')), parts along dimension 0
The draws below stay inside these ranges and needn't reach their ends.
There are 2 independent parts, one for each index of `groups`. The reference program is written for one: setup_inputs(seed, part) draws one part's arguments, and reference() takes and returns one part's arrays. A program takes and returns all parts, laid end to end along the dimension named above; an argument that names none is the same for every part. Nothing has to cross between parts.
All inputs are finite; a program needn't handle non-finite values.
Results may differ from the reference program's by a relative error of at most 0.0049.
Values may be sent and summed in bfloat16 or wider, within the bound.
No kernel may reach another device: no remote copies, remote signals or barrier semaphores. Data moves between devices by JAX's collectives and lax.ppermute only.
A program may use at most 128 MiB of HBM per device.

```python
import jax
import jax.numpy as jnp
from jax import lax

D = 8192
FF = 14336
TOKENS = 128


def shard_levels(own_key, dims, cuts, smallest, top_value):
    factor_of = 1.0
    for dim, blocks in cuts:
        steps = jax.random.uniform(jax.random.fold_in(jax.random.fold_in(own_key, 6), dim), (blocks,), jnp.float32, smallest / len(cuts), top_value / len(cuts))
        factor_of = factor_of * jnp.repeat(jnp.exp(steps), dims[dim] // blocks).reshape((-1,) + (1,) * (len(dims) - 1 - dim))
    return factor_of


def bell_draw(own_key, shape, spread, most, cuts=(), kind=jnp.bfloat16):
    factor_of = shard_levels(own_key, shape, cuts, -0.22, 0.18) if cuts else 1.0
    array = jax.random.normal(own_key, shape, jnp.float32) * spread * factor_of
    return jnp.minimum(jnp.maximum(array, -most), most).astype(kind)


def setup_inputs(seed: int = 0, part: int = 0) -> dict:
    key_list = jax.random.split(jax.random.key(seed), 6)
    own_keys = jax.random.split(jax.random.fold_in(key_list[5], part), 6)
    tokens = bell_draw(own_keys[0], (TOKENS, D), 1.0, 6.0, ((0, 16),))
    norm_gain = jnp.clip(1.0 + 0.15 * jax.random.normal(key_list[1], (D,), jnp.float32), 0.25, 1.75)
    gate_weight = bell_draw(key_list[2], (D, FF), D ** -0.5, 0.0625, ((1, 16),))
    up_weight = bell_draw(key_list[3], (D, FF), D ** -0.5, 0.0625, ((1, 16),))
    down_weight = bell_draw(key_list[4], (FF, D), FF ** -0.5, 0.046875, ((0, 16),))
    return dict(tokens=tokens, norm_gain=norm_gain, gate_weight=gate_weight, up_weight=up_weight, down_weight=down_weight)


def reference(tokens, norm_gain, gate_weight, up_weight, down_weight):
    widened = tokens.astype(jnp.float32)
    inv_rms = jax.lax.rsqrt(lax.optimization_barrier(jnp.mean(widened * widened, axis=-1, keepdims=True)) + 1e-05)
    normed = (widened * inv_rms * norm_gain).astype(jnp.bfloat16)
    gate_out = jnp.dot(normed, gate_weight, preferred_element_type=jnp.float32)
    up_out = jnp.dot(normed, up_weight, preferred_element_type=jnp.float32)
    hidden = (jax.nn.silu(gate_out) * up_out).astype(jnp.bfloat16)
    summed = jnp.dot(hidden, down_weight, preferred_element_type=jnp.float32)
    return (widened + summed).astype(jnp.bfloat16)
```

```python
import functools

import jax
import jax.numpy as jnp
from jax import lax
from jax.experimental import pallas as pl
from jax.experimental.pallas import tpu as pltpu
from jax.sharding import PartitionSpec as P

BF = jnp.bfloat16
F32 = jnp.float32
N_CHUNKS = 2
PARTS = 4
HELD = 2


def flip(x, axis, size, mask):
    return lax.ppermute(x, axis, [(i, i ^ mask) for i in range(size)])


def norm_rows(tokens, norm_gain):
    widened = tokens.astype(F32)
    inv_rms = lax.rsqrt(jnp.mean(widened * widened, axis=-1, keepdims=True) + 1e-05)
    return (widened * inv_rms * norm_gain).astype(BF)


def vmem_specs(count):
    return [pl.BlockSpec(memory_space=pltpu.VMEM)] * count


def norm_kernel(tokens, gain, out):
    out[...] = norm_rows(tokens[...], gain[...])


def fetch_kernel(part, parts, gate, up, gate_out, up_out, mark, sems):
    depth = gate_out.shape[0]
    copies = [
        pltpu.make_async_copy(src.at[pl.ds(part * depth, depth)], dst, sems.at[i])
        for i, (src, dst) in enumerate([(gate, gate_out), (up, up_out)])
    ]
    for copy in copies:
        copy.start()
    mark[...] = jnp.zeros_like(mark)
    for copy in copies:
        copy.wait()


def fetch(gate, up, part, parts):
    depth, units = gate.shape[0] // parts, gate.shape[1]
    return pl.pallas_call(
        functools.partial(fetch_kernel, part, parts),
        out_shape=[pltpu.VMEM((depth, units), BF)] * 2 + [jax.ShapeDtypeStruct((16, 128), BF)],
        in_specs=[pl.BlockSpec(memory_space=pltpu.HBM)] * 2,
        out_specs=vmem_specs(3),
        scratch_shapes=[pltpu.SemaphoreType.DMA((2,))],
        compiler_params=pltpu.CompilerParams(vmem_limit_bytes=1 * 2**20),
        cost_estimate=pl.CostEstimate(flops=0, bytes_accessed=4 * depth * units, transcendentals=0),
        name=f"fetch_{part}",
    )(hbm(gate), hbm(up))


def hidden_kernel(held, parts, *refs):
    pieces, rest = refs[:16], refs[16:]
    gates, ups, (gate, up, out, gate_late, up_late, sems) = rest[:held], rest[held : 2 * held], rest[2 * held :]
    depth = gate.shape[0] // parts
    copies = []
    for k in range(held, parts):
        for i, (src, dst) in enumerate([(gate, gate_late), (up, up_late)]):
            copies.append(pltpu.make_async_copy(src.at[pl.ds(k * depth, depth)], dst.at[k - held], sems.at[k - held, i]))
            copies[-1].start()
    gate_out = up_out = 0.0
    for k in range(parts):
        rows = jnp.concatenate([p[:, k * depth : (k + 1) * depth] for p in pieces], axis=0)
        if k >= held:
            copies[2 * (k - held)].wait()
            copies[2 * (k - held) + 1].wait()
        gate_block = gates[k][...] if k < held else gate_late[k - held]
        up_block = ups[k][...] if k < held else up_late[k - held]
        gate_out += jnp.dot(rows, gate_block, preferred_element_type=F32)
        up_out += jnp.dot(rows, up_block, preferred_element_type=F32)
    out[...] = (jax.nn.silu(gate_out) * up_out).astype(BF)


def down_kernel(hidden, down, own, other):
    half = own.shape[0]
    part = jnp.dot(hidden[...], down[...], preferred_element_type=F32)
    own[...] = part[:half]
    other[...] = part[half:].astype(BF)


def pair_kernel(chunks, depth, *refs):
    owns, recvs, keeps, sends = refs[:chunks], refs[chunks : 2 * chunks], refs[2 * chunks : 2 * chunks + depth], refs[2 * chunks + depth :]
    rows = keeps[0].shape[0]
    for c in range(chunks):
        step = owns[c].shape[1]
        cols = slice(c * step, (c + 1) * step)
        total = owns[c][...] + recvs[c][...].astype(F32)
        for d in range(depth):
            keeps[d][:, cols] = total[d * rows : (d + 1) * rows]
            sends[d][:, cols] = total[(depth + d) * rows : (depth + d + 1) * rows].astype(BF)


def hbm(x):
    return pltpu.with_memory_space_constraint(x, pltpu.HBM)


def tie(x, mark):
    return x + mark[0, 0]


def pin(x):
    return pltpu.with_memory_space_constraint(x, pltpu.VMEM)


def per_device(tokens, norm_gain, gate_weight, up_weight, down_weight):
    rows, width = tokens.shape
    units = gate_weight.shape[1]
    depth = 4
    normed = pl.pallas_call(
        norm_kernel,
        out_shape=jax.ShapeDtypeStruct((rows, width), BF),
        in_specs=vmem_specs(2),
        out_specs=vmem_specs(1)[0],
        name="norm",
    )(tokens, norm_gain.reshape(1, width))
    z_pieces = [normed] + [flip(normed, "tensor", 8, 2 * d) for d in range(1, depth)]
    fetched = [fetch(gate_weight, up_weight, i, PARTS) for i in range(PARTS)]
    fetched = [fetch(gate_weight, up_weight, i, PARTS) for i in range(HELD)]
    y_pieces = [flip(normed, "tensor", 8, 1)]
    for d in range(1, depth):
        y_pieces.append(flip(tie(z_pieces[d], fetched[min(d, HELD) - 1][2]), "tensor", 8, 1))
    mine = z_pieces + y_pieces
    pieces = mine + [flip(p, "dp", 2, 1) for p in mine]
    late = (PARTS - HELD, width // PARTS, units)
    hidden = pl.pallas_call(
        functools.partial(hidden_kernel, HELD, PARTS),
        out_shape=jax.ShapeDtypeStruct((16 * rows, units), BF),
        in_specs=vmem_specs(16 + 2 * HELD) + [pl.BlockSpec(memory_space=pltpu.HBM)] * 2,
        out_specs=vmem_specs(1)[0],
        scratch_shapes=[pltpu.VMEM(late, BF), pltpu.VMEM(late, BF), pltpu.SemaphoreType.DMA((PARTS - HELD, 2))],
        compiler_params=pltpu.CompilerParams(vmem_limit_bytes=24 * 2**20),
        name="hidden",
    )(*pieces, *[pin(f[0]) for f in fetched], *[pin(f[1]) for f in fetched], hbm(gate_weight), hbm(up_weight))
    step = width // N_CHUNKS
    owns, recvs = [], []
    for c in range(N_CHUNKS):
        own, other = pl.pallas_call(
            down_kernel,
            out_shape=(jax.ShapeDtypeStruct((8 * rows, step), F32), jax.ShapeDtypeStruct((8 * rows, step), BF)),
            grid=(1,),
            in_specs=[pl.BlockSpec((16 * rows, units), lambda i: (0, 0)), pl.BlockSpec((units, step), functools.partial(lambda c, i: (0, c), c))],
            out_specs=(pl.BlockSpec((8 * rows, step), lambda i: (0, 0)),) * 2,
            compiler_params=pltpu.CompilerParams(vmem_limit_bytes=16 * 2**20),
            name="down",
        )(hidden, down_weight)
        owns.append(own)
        recvs.append(flip(other, "dp", 2, 1))
    pairs = pl.pallas_call(
        functools.partial(pair_kernel, N_CHUNKS, depth),
        out_shape=[jax.ShapeDtypeStruct((rows, width), F32)] * depth + [jax.ShapeDtypeStruct((rows, width), BF)] * depth,
        in_specs=vmem_specs(2 * N_CHUNKS),
        out_specs=vmem_specs(2 * depth),
        compiler_params=pltpu.CompilerParams(vmem_limit_bytes=16 * 2**20),
        name="pair",
    )(*owns, *recvs)
    keeps, sends = pairs[:depth], pairs[depth:]
    total = tokens.astype(F32)
    sums = {}
    for d in reversed(range(depth)):
        sums[d] = keeps[d] + flip(sends[d], "tensor", 8, 1).astype(F32)
        if d:
            sums[d] = flip(sums[d].astype(BF), "tensor", 8, 2 * d).astype(F32)
    for d in range(depth):
        total = total + sums[d]
    return total.astype(BF)


def generic_device(tokens, norm_gain, gate_weight, up_weight, down_weight):
    normed = norm_rows(tokens, norm_gain)
    gathered = lax.all_gather(normed, ("dp", "tensor"), axis=0, tiled=True)
    gate_out = jnp.dot(gathered, gate_weight, preferred_element_type=F32)
    up_out = jnp.dot(gathered, up_weight, preferred_element_type=F32)
    hidden = (jax.nn.silu(gate_out) * up_out).astype(BF)
    partial = jnp.dot(hidden, down_weight, preferred_element_type=F32)
    summed = lax.psum_scatter(partial, ("dp", "tensor"), scatter_dimension=0, tiled=True)
    return (tokens.astype(F32) + summed).astype(BF)


def solution(mesh):
    tuned = mesh.shape["dp"] == 2 and mesh.shape["tensor"] == 8
    in_specs = (
        P(("groups", "dp", "tensor"), None),
        P(),
        P(None, ("dp", "tensor")),
        P(None, ("dp", "tensor")),
        P(("dp", "tensor"), None),
    )
    out_specs = P(("groups", "dp", "tensor"), None)
    return jax.shard_map(
        per_device if tuned else generic_device, mesh=mesh, in_specs=in_specs, out_specs=out_specs, check_vma=False
    )
```

```python
import functools

import jax
import jax.numpy as jnp
from jax import lax
from jax.experimental import pallas as pl
from jax.experimental.pallas import tpu as pltpu
from jax.sharding import PartitionSpec as P

BF = jnp.bfloat16
F32 = jnp.float32
N_CHUNKS = 2
COST = 4
FETCHES = (4, 2)
CHUNK = 1024
ORDER = (0, 2, 3, 6, 1, 5, 7, 4)


def flip(x, axis, size, mask):
    return lax.ppermute(x, axis, [(i, i ^ mask) for i in range(size)])


def norm_rows(tokens, norm_gain):
    widened = tokens.astype(F32)
    inv_rms = lax.rsqrt(jnp.mean(widened * widened, axis=-1, keepdims=True) + 1e-05)
    return (widened * inv_rms * norm_gain).astype(BF)


def vmem_specs(count):
    return [pl.BlockSpec(memory_space=pltpu.VMEM)] * count


def norm_kernel(tokens, gain, out):
    out[...] = norm_rows(tokens[...], gain[...])


def fetch_kernel(first, after, *refs):
    gate, up = refs[:2]
    gate_out, up_out, mark, sems = refs[2 + after :]
    depth = gate_out.shape[0]
    copies = [
        pltpu.make_async_copy(src.at[pl.ds(first, depth)], dst, sems.at[i])
        for i, (src, dst) in enumerate([(gate, gate_out), (up, up_out)])
    ]
    for copy in copies:
        copy.start()
    mark[...] = jnp.zeros_like(mark)
    for copy in copies:
        copy.wait()


def fetch(gate, up, first, depth, shape, after):
    units = gate.shape[1]
    return pl.pallas_call(
        functools.partial(fetch_kernel, first, len(after)),
        out_shape=[pltpu.VMEM((depth, units), BF)] * 2 + [pltpu.VMEM(shape, BF)],
        in_specs=[pl.BlockSpec(memory_space=pltpu.HBM)] * 2 + [pl.BlockSpec(memory_space=pl.ANY)] * len(after),
        out_specs=vmem_specs(3),
        scratch_shapes=[pltpu.SemaphoreType.DMA((2,))],
        compiler_params=pltpu.CompilerParams(vmem_limit_bytes=1 * 2**20),
        cost_estimate=pl.CostEstimate(flops=0, bytes_accessed=COST * depth * units, transcendentals=0),
        name=f"fetch_{first}",
    )(hbm(gate), hbm(up), *after)


def hidden_kernel(held, *refs):
    pieces, rest = refs[:16], refs[16:]
    gates, ups, (gate, up, out, gate_late, up_late, sems) = rest[:held], rest[held : 2 * held], rest[2 * held :]
    late, depth = gate_late.shape[:2]
    base = gate.shape[0] - late * depth
    copies = []
    for k in range(late):
        for i, (src, dst) in enumerate([(gate, gate_late), (up, up_late)]):
            copies.append(pltpu.make_async_copy(src.at[pl.ds(base + k * depth, depth)], dst.at[k], sems.at[k, i]))
            copies[-1].start()
    gate_out = up_out = 0.0
    first = 0
    for k in range(held + late):
        size = gates[k].shape[0] if k < held else depth
        rows = jnp.concatenate([p[:, first : first + size] for p in pieces], axis=0)
        if k >= held:
            copies[2 * (k - held)].wait()
            copies[2 * (k - held) + 1].wait()
        gate_block = gates[k][...] if k < held else gate_late[k - held]
        up_block = ups[k][...] if k < held else up_late[k - held]
        gate_out += jnp.dot(rows, gate_block, preferred_element_type=F32)
        up_out += jnp.dot(rows, up_block, preferred_element_type=F32)
        first += size
    out[...] = (jax.nn.silu(gate_out) * up_out).astype(BF)


def down_kernel(hidden, down, own, other):
    half = own.shape[0]
    part = jnp.dot(hidden[...], down[...], preferred_element_type=F32)
    own[...] = part[:half]
    other[...] = part[half:].astype(BF)


def pair_kernel(chunks, *refs):
    owns, recvs, outs = refs[:chunks], refs[chunks : 2 * chunks], refs[2 * chunks :]
    rows = outs[0].shape[0]
    for c in range(chunks):
        step = owns[c].shape[1]
        total = owns[c][...] + recvs[c][...].astype(F32)
        for d, out in enumerate(outs):
            out[:, c * step : (c + 1) * step] = total[d * rows : (d + 1) * rows].astype(out.dtype)


def hbm(x):
    return pltpu.with_memory_space_constraint(x, pltpu.HBM)


def tie(x, mark):
    return x + mark


def pin(x):
    return pltpu.with_memory_space_constraint(x, pltpu.VMEM)


def per_device(tokens, norm_gain, gate_weight, up_weight, down_weight):
    rows, width = tokens.shape
    units = gate_weight.shape[1]
    normed = pl.pallas_call(
        norm_kernel,
        out_shape=pltpu.VMEM((rows, width), BF),
        in_specs=vmem_specs(2),
        out_specs=vmem_specs(1)[0],
        name="norm",
    )(tokens, norm_gain.reshape(1, width))

    def hop(x, mask):
        return flip(x, "tensor", 8, mask)

    sizes = [CHUNK * n for n in FETCHES]
    at1, at2, at4 = hop(normed, 1), hop(normed, 2), hop(normed, 4)
    early = fetch(gate_weight, up_weight, 0, sizes[0], tokens.shape, [at1, at2])
    at4t = tie(at4, early[2])
    at7, at3 = hop(at1, 6), hop(at2, 1)
    at6, at5 = hop(at4t, 2), hop(at4t, 1)
    later = fetch(gate_weight, up_weight, sizes[0], sizes[1], tokens.shape, [at4])
    mine = [normed, at1, at2, at4]
    last = [at7, at3, at6, at5]
    pieces = mine + last
    pieces += [flip(p, "dp", 2, 1) for p in mine + [tie(p, later[2]) for p in last]]
    held = [early, later]
    pieces = [pieces[i] for i in ORDER] + [pieces[8 + i] for i in ORDER]
    late = ((width - sum(sizes)) // CHUNK, CHUNK, units)
    hidden = pl.pallas_call(
        functools.partial(hidden_kernel, len(held)),
        out_shape=jax.ShapeDtypeStruct((16 * rows, units), BF),
        in_specs=vmem_specs(16 + 2 * len(held)) + [pl.BlockSpec(memory_space=pltpu.HBM)] * 2,
        out_specs=vmem_specs(1)[0],
        scratch_shapes=[pltpu.VMEM(late, BF), pltpu.VMEM(late, BF), pltpu.SemaphoreType.DMA((late[0], 2))],
        compiler_params=pltpu.CompilerParams(vmem_limit_bytes=24 * 2**20),
        name="hidden",
    )(*pieces, *[pin(f[0]) for f in held], *[pin(f[1]) for f in held], hbm(gate_weight), hbm(up_weight))
    step = width // N_CHUNKS
    owns, recvs = [], []
    for c in range(N_CHUNKS):
        own, other = pl.pallas_call(
            down_kernel,
            out_shape=(jax.ShapeDtypeStruct((8 * rows, step), F32), jax.ShapeDtypeStruct((8 * rows, step), BF)),
            grid=(1,),
            in_specs=[pl.BlockSpec((16 * rows, units), lambda i: (0, 0)), pl.BlockSpec((units, step), functools.partial(lambda c, i: (0, c), c))],
            out_specs=(pl.BlockSpec((8 * rows, step), lambda i: (0, 0)),) * 2,
            compiler_params=pltpu.CompilerParams(vmem_limit_bytes=16 * 2**20),
            name="down",
        )(hidden, down_weight)
        owns.append(own)
        recvs.append(flip(other, "dp", 2, 1))
    kinds = [F32, F32, F32, BF, F32, BF, BF, BF]
    own0, own1, own2, own3, far0, far1, far2, far3 = pl.pallas_call(
        functools.partial(pair_kernel, N_CHUNKS),
        out_shape=[jax.ShapeDtypeStruct((rows, width), kind) for kind in kinds],
        in_specs=vmem_specs(2 * N_CHUNKS),
        out_specs=vmem_specs(8),
        compiler_params=pltpu.CompilerParams(vmem_limit_bytes=16 * 2**20),
        name="pair",
    )(*owns, *recvs)

    def send(x, mask):
        return flip(x.astype(BF), "tensor", 8, mask).astype(F32)

    sum2 = own2 + send(far2, 1) + send(own3, 2)
    sum0 = far0 + send(far3, 6)
    sum1 = own1 + send(far1, 1)
    total = own0 + send(sum2, 4) + send(sum0, 1) + send(sum1, 2)
    return (tokens.astype(F32) + total).astype(BF)


def generic_device(tokens, norm_gain, gate_weight, up_weight, down_weight):
    normed = norm_rows(tokens, norm_gain)
    gathered = lax.all_gather(normed, ("dp", "tensor"), axis=0, tiled=True)
    gate_out = jnp.dot(gathered, gate_weight, preferred_element_type=F32)
    up_out = jnp.dot(gathered, up_weight, preferred_element_type=F32)
    hidden = (jax.nn.silu(gate_out) * up_out).astype(BF)
    partial = jnp.dot(hidden, down_weight, preferred_element_type=F32)
    summed = lax.psum_scatter(partial, ("dp", "tensor"), scatter_dimension=0, tiled=True)
    return (tokens.astype(F32) + summed).astype(BF)


def solution(mesh):
    tuned = mesh.shape["dp"] == 2 and mesh.shape["tensor"] == 8
    in_specs = (
        P(("groups", "dp", "tensor"), None),
        P(),
        P(None, ("dp", "tensor")),
        P(None, ("dp", "tensor")),
        P(("dp", "tensor"), None),
    )
    out_specs = P(("groups", "dp", "tensor"), None)
    return jax.shard_map(
        per_device if tuned else generic_device, mesh=mesh, in_specs=in_specs, out_specs=out_specs, check_vma=False
    )
```

```python
import functools

import jax
import jax.numpy as jnp
from jax import lax
from jax.experimental import pallas as pl
from jax.experimental.pallas import tpu as pltpu
from jax.sharding import PartitionSpec as P

BF = jnp.bfloat16
F32 = jnp.float32
SPLIT = (3, 1)
COST = 4
FETCHES = (4, 2)
CHUNK = 1024
ORDER = (0, 2, 3, 6, 1, 5, 7, 4)


def flip(x, axis, size, mask):
    return lax.ppermute(x, axis, [(i, i ^ mask) for i in range(size)])


def inverse_rms(rows):
    widened = rows.astype(F32)
    return lax.rsqrt(jnp.mean(widened * widened, axis=-1, keepdims=True) + 1e-05)


def scaled(rows, inv_rms, gain):
    return (rows.astype(F32) * inv_rms * gain).astype(BF)


def vmem_specs(count):
    return [pl.BlockSpec(memory_space=pltpu.VMEM)] * count


def fetch_kernel(first, after, *refs):
    gate, up = refs[:2]
    gate_out, up_out, mark, sems = refs[2 + after :]
    depth = gate_out.shape[0]
    copies = [
        pltpu.make_async_copy(src.at[pl.ds(first, depth)], dst, sems.at[i])
        for i, (src, dst) in enumerate([(gate, gate_out), (up, up_out)])
    ]
    for copy in copies:
        copy.start()
    mark[...] = jnp.zeros_like(mark)
    for copy in copies:
        copy.wait()


def fetch(gate, up, first, depth, shape, after):
    units = gate.shape[1]
    return pl.pallas_call(
        functools.partial(fetch_kernel, first, len(after)),
        out_shape=[pltpu.VMEM((depth, units), BF)] * 2 + [pltpu.VMEM(shape, BF)],
        in_specs=[pl.BlockSpec(memory_space=pltpu.HBM)] * 2 + [pl.BlockSpec(memory_space=pl.ANY)] * len(after),
        out_specs=vmem_specs(3),
        scratch_shapes=[pltpu.SemaphoreType.DMA((2,))],
        compiler_params=pltpu.CompilerParams(vmem_limit_bytes=1 * 2**20),
        cost_estimate=pl.CostEstimate(flops=0, bytes_accessed=COST * depth * units, transcendentals=0),
        name=f"fetch_{first}",
    )(hbm(gate), hbm(up), *after)


def hidden_kernel(held, *refs):
    pieces, gain, rest = refs[:16], refs[16], refs[17:]
    gates, ups, (gate, up, out, gate_late, up_late, sems) = rest[:held], rest[held : 2 * held], rest[2 * held :]
    late, depth = gate_late.shape[:2]
    base = gate.shape[0] - late * depth
    copies = []
    for k in range(late):
        for i, (src, dst) in enumerate([(gate, gate_late), (up, up_late)]):
            copies.append(pltpu.make_async_copy(src.at[pl.ds(base + k * depth, depth)], dst.at[k], sems.at[k, i]))
            copies[-1].start()
    inv_rms = [inverse_rms(p[...]) for p in pieces]
    gate_out = up_out = 0.0
    first = 0
    for k in range(held + late):
        size = gates[k].shape[0] if k < held else depth
        cols = slice(first, first + size)
        rows = jnp.concatenate([scaled(p[:, cols], inv, gain[:, cols]) for p, inv in zip(pieces, inv_rms)], axis=0)
        if k >= held:
            copies[2 * (k - held)].wait()
            copies[2 * (k - held) + 1].wait()
        gate_block = gates[k][...] if k < held else gate_late[k - held]
        up_block = ups[k][...] if k < held else up_late[k - held]
        gate_out += jnp.dot(rows, gate_block, preferred_element_type=F32)
        up_out += jnp.dot(rows, up_block, preferred_element_type=F32)
        first += size
    out[...] = (jax.nn.silu(gate_out) * up_out).astype(BF)


def down_kernel(hidden, down, own, other):
    half = own.shape[0]
    part = jnp.dot(hidden[...], down[...], preferred_element_type=F32)
    own[...] = part[:half]
    other[...] = part[half:].astype(BF)


def pair_kernel(chunks, *refs):
    owns, recvs, outs = refs[:chunks], refs[chunks : 2 * chunks], refs[2 * chunks :]
    rows = outs[0].shape[0]
    first = 0
    for c in range(chunks):
        step = owns[c].shape[1]
        total = owns[c][...] + recvs[c][...].astype(F32)
        for d, out in enumerate(outs):
            out[:, first : first + step] = total[d * rows : (d + 1) * rows].astype(out.dtype)
        first += step


def hbm(x):
    return pltpu.with_memory_space_constraint(x, pltpu.HBM)


def tie(x, mark):
    return x + mark


def pin(x):
    return pltpu.with_memory_space_constraint(x, pltpu.VMEM)


def per_device(tokens, norm_gain, gate_weight, up_weight, down_weight):
    rows, width = tokens.shape
    units = gate_weight.shape[1]
    def hop(x, mask):
        return flip(x, "tensor", 8, mask)

    sizes = [CHUNK * n for n in FETCHES]
    at1, at2, at4 = hop(tokens, 1), hop(tokens, 2), hop(tokens, 4)
    early = fetch(gate_weight, up_weight, 0, sizes[0], tokens.shape, [at1, at2])
    at4t = tie(at4, early[2])
    at7, at3 = hop(at1, 6), hop(at2, 1)
    at6, at5 = hop(at4t, 2), hop(at4t, 1)
    later = fetch(gate_weight, up_weight, sizes[0], sizes[1], tokens.shape, [at4])
    mine = [tokens, at1, at2, at4]
    last = [at7, at3, at6, at5]
    pieces = mine + last
    pieces += [flip(p, "dp", 2, 1) for p in mine + [tie(p, later[2]) for p in last]]
    held = [early, later]
    pieces = [pieces[i] for i in ORDER] + [pieces[8 + i] for i in ORDER]
    late = ((width - sum(sizes)) // CHUNK, CHUNK, units)
    hidden = pl.pallas_call(
        functools.partial(hidden_kernel, len(held)),
        out_shape=jax.ShapeDtypeStruct((16 * rows, units), BF),
        in_specs=vmem_specs(17 + 2 * len(held)) + [pl.BlockSpec(memory_space=pltpu.HBM)] * 2,
        out_specs=vmem_specs(1)[0],
        scratch_shapes=[pltpu.VMEM(late, BF), pltpu.VMEM(late, BF), pltpu.SemaphoreType.DMA((late[0], 2))],
        compiler_params=pltpu.CompilerParams(vmem_limit_bytes=24 * 2**20),
        name="hidden",
    )(*pieces, norm_gain.reshape(1, width), *[pin(f[0]) for f in held], *[pin(f[1]) for f in held], hbm(gate_weight), hbm(up_weight))
    first, unit = 0, width // sum(SPLIT)
    owns, recvs = [], []
    for share in SPLIT:
        step = share * unit
        own, other = pl.pallas_call(
            down_kernel,
            out_shape=(jax.ShapeDtypeStruct((8 * rows, step), F32), jax.ShapeDtypeStruct((8 * rows, step), BF)),
            grid=(1,),
            in_specs=[pl.BlockSpec((16 * rows, units), lambda i: (0, 0)), pl.BlockSpec((units, step), functools.partial(lambda c, i: (0, c), first // step))],
            out_specs=(pl.BlockSpec((8 * rows, step), lambda i: (0, 0)),) * 2,
            compiler_params=pltpu.CompilerParams(vmem_limit_bytes=20 * 2**20),
            name="down",
        )(hidden, down_weight)
        owns.append(own)
        recvs.append(flip(other, "dp", 2, 1))
        first += step
    kinds = [F32, F32, F32, BF, F32, BF, BF, BF]
    own0, own1, own2, own3, far0, far1, far2, far3 = pl.pallas_call(
        functools.partial(pair_kernel, len(SPLIT)),
        out_shape=[jax.ShapeDtypeStruct((rows, width), kind) for kind in kinds],
        in_specs=vmem_specs(2 * len(SPLIT)),
        out_specs=vmem_specs(8),
        compiler_params=pltpu.CompilerParams(vmem_limit_bytes=16 * 2**20),
        name="pair",
    )(*owns, *recvs)

    def send(x, mask):
        return flip(x.astype(BF), "tensor", 8, mask).astype(F32)

    sum2 = own2 + send(far2, 1) + send(own3, 2)
    sum0 = far0 + send(far3, 6)
    sum1 = own1 + send(far1, 1)
    total = own0 + send(sum2, 4) + send(sum0, 1) + send(sum1, 2)
    return (tokens.astype(F32) + total).astype(BF)


def generic_device(tokens, norm_gain, gate_weight, up_weight, down_weight):
    normed = scaled(tokens, inverse_rms(tokens), norm_gain)
    gathered = lax.all_gather(normed, ("dp", "tensor"), axis=0, tiled=True)
    gate_out = jnp.dot(gathered, gate_weight, preferred_element_type=F32)
    up_out = jnp.dot(gathered, up_weight, preferred_element_type=F32)
    hidden = (jax.nn.silu(gate_out) * up_out).astype(BF)
    partial = jnp.dot(hidden, down_weight, preferred_element_type=F32)
    summed = lax.psum_scatter(partial, ("dp", "tensor"), scatter_dimension=0, tiled=True)
    return (tokens.astype(F32) + summed).astype(BF)


def solution(mesh):
    tuned = mesh.shape["dp"] == 2 and mesh.shape["tensor"] == 8
    in_specs = (
        P(("groups", "dp", "tensor"), None),
        P(),
        P(None, ("dp", "tensor")),
        P(None, ("dp", "tensor")),
        P(("dp", "tensor"), None),
    )
    out_specs = P(("groups", "dp", "tensor"), None)
    return jax.shard_map(
        per_device if tuned else generic_device, mesh=mesh, in_specs=in_specs, out_specs=out_specs, check_vma=False
    )
```

```python
import functools

import jax
import jax.numpy as jnp
from jax import lax
from jax.experimental import pallas as pl
from jax.experimental.pallas import tpu as pltpu
from jax.sharding import PartitionSpec as P

BF = jnp.bfloat16
F32 = jnp.float32
SPLIT = (3, 1)
COST = 4
FETCHES = (2, 4)
CHUNK = 1024
ORDER = (0, 2, 3, 6, 1, 5, 7, 4)


def flip(x, axis, size, mask):
    return lax.ppermute(x, axis, [(i, i ^ mask) for i in range(size)])


def inverse_rms(rows):
    widened = rows.astype(F32)
    return lax.rsqrt(jnp.mean(widened * widened, axis=-1, keepdims=True) + 1e-05)


def scaled(rows, inv_rms, gain):
    return (rows.astype(F32) * inv_rms * gain).astype(BF)


def vmem_specs(count):
    return [pl.BlockSpec(memory_space=pltpu.VMEM)] * count


def fetch_kernel(first, after, *refs):
    gate, up = refs[:2]
    gate_out, up_out, mark, sems = refs[2 + after :]
    depth = gate_out.shape[0]
    copies = [
        pltpu.make_async_copy(src.at[pl.ds(first, depth)], dst, sems.at[i])
        for i, (src, dst) in enumerate([(gate, gate_out), (up, up_out)])
    ]
    for copy in copies:
        copy.start()
    mark[...] = jnp.zeros_like(mark)
    for copy in copies:
        copy.wait()


def fetch(gate, up, first, depth, shape, after):
    units = gate.shape[1]
    return pl.pallas_call(
        functools.partial(fetch_kernel, first, len(after)),
        out_shape=[pltpu.VMEM((depth, units), BF)] * 2 + [pltpu.VMEM(shape, BF)],
        in_specs=[pl.BlockSpec(memory_space=pltpu.HBM)] * 2 + [pl.BlockSpec(memory_space=pl.ANY)] * len(after),
        out_specs=vmem_specs(3),
        scratch_shapes=[pltpu.SemaphoreType.DMA((2,))],
        compiler_params=pltpu.CompilerParams(vmem_limit_bytes=1 * 2**20),
        cost_estimate=pl.CostEstimate(flops=0, bytes_accessed=COST * depth * units, transcendentals=0),
        name=f"fetch_{first}",
    )(hbm(gate), hbm(up), *after)


def hidden_kernel(held, *refs):
    near, (far_last, gain), rest = refs[:12], refs[12:14], refs[14:]
    pieces = list(near) + [far_last.at[8 * i : 8 * i + 8] for i in range(4)]
    pieces = [pieces[i] for i in ORDER + tuple(8 + i for i in ORDER)]
    gates, ups, (gate, up, out, gate_late, up_late, sems) = rest[:held], rest[held : 2 * held], rest[2 * held :]
    late, depth = gate_late.shape[:2]
    base = gate.shape[0] - late * depth
    copies = []
    for k in range(late):
        for i, (src, dst) in enumerate([(gate, gate_late), (up, up_late)]):
            copies.append(pltpu.make_async_copy(src.at[pl.ds(base + k * depth, depth)], dst.at[k], sems.at[k, i]))
            copies[-1].start()
    inv_rms = [inverse_rms(p[...]) for p in pieces]
    gate_out = up_out = 0.0
    first = 0
    for k in range(held + late):
        size = gates[k].shape[0] if k < held else depth
        cols = slice(first, first + size)
        rows = jnp.concatenate([scaled(p[:, cols], inv, gain[:, cols]) for p, inv in zip(pieces, inv_rms)], axis=0)
        if k >= held:
            copies[2 * (k - held)].wait()
            copies[2 * (k - held) + 1].wait()
        gate_block = gates[k][...] if k < held else gate_late[k - held]
        up_block = ups[k][...] if k < held else up_late[k - held]
        gate_out += jnp.dot(rows, gate_block, preferred_element_type=F32)
        up_out += jnp.dot(rows, up_block, preferred_element_type=F32)
        first += size
    out[...] = (jax.nn.silu(gate_out) * up_out).astype(BF)


def down_kernel(hidden, down, own, other):
    half = own.shape[0]
    part = jnp.dot(hidden[...], down[...], preferred_element_type=F32)
    own[...] = part[:half]
    other[...] = part[half:].astype(BF)


def pair_kernel(chunks, *refs):
    owns, recvs, outs = refs[:chunks], refs[chunks : 2 * chunks], refs[2 * chunks :]
    rows = outs[0].shape[0]
    first = 0
    for c in range(chunks):
        step = owns[c].shape[1]
        total = owns[c][...] + recvs[c][...].astype(F32)
        for d, out in enumerate(outs):
            out[:, first : first + step] = total[d * rows : (d + 1) * rows].astype(out.dtype)
        first += step


def hbm(x):
    return pltpu.with_memory_space_constraint(x, pltpu.HBM)


def tie(x, mark):
    return x + mark


def pin(x):
    return pltpu.with_memory_space_constraint(x, pltpu.VMEM)


def per_device(tokens, norm_gain, gate_weight, up_weight, down_weight):
    rows, width = tokens.shape
    units = gate_weight.shape[1]
    def hop(x, mask):
        return flip(x, "tensor", 8, mask)

    sizes = [CHUNK * n for n in FETCHES]
    at1, at2, at4 = hop(tokens, 1), hop(tokens, 2), hop(tokens, 4)
    early = fetch(gate_weight, up_weight, 0, sizes[0], tokens.shape, [])
    at4t = tie(at4, early[2])
    at7, at3 = hop(tie(at1, early[2]), 6), hop(tie(at2, early[2]), 1)
    at6, at5 = hop(at4t, 2), hop(at4t, 1)
    later = fetch(gate_weight, up_weight, sizes[0], sizes[1], tokens.shape, [at4])
    mine = [tokens, at1, at2, at4]
    last = [at7, at3, at6, at5]
    far_mine = [flip(p, "dp", 2, 1) for p in mine]
    far_last = flip(jnp.concatenate([tie(p, later[2]) for p in last], axis=0), "dp", 2, 1)
    held = [early, later]
    pieces = mine + last + far_mine + [far_last]
    late = ((width - sum(sizes)) // CHUNK, CHUNK, units)
    hidden = pl.pallas_call(
        functools.partial(hidden_kernel, len(held)),
        out_shape=jax.ShapeDtypeStruct((16 * rows, units), BF),
        in_specs=vmem_specs(14 + 2 * len(held)) + [pl.BlockSpec(memory_space=pltpu.HBM)] * 2,
        out_specs=vmem_specs(1)[0],
        scratch_shapes=[pltpu.VMEM(late, BF), pltpu.VMEM(late, BF), pltpu.SemaphoreType.DMA((late[0], 2))],
        compiler_params=pltpu.CompilerParams(vmem_limit_bytes=24 * 2**20),
        name="hidden",
    )(*pieces, norm_gain.reshape(1, width), *[pin(f[0]) for f in held], *[pin(f[1]) for f in held], hbm(gate_weight), hbm(up_weight))
    first, unit = 0, width // sum(SPLIT)
    owns, recvs = [], []
    for share in SPLIT:
        step = share * unit
        own, other = pl.pallas_call(
            down_kernel,
            out_shape=(jax.ShapeDtypeStruct((8 * rows, step), F32), jax.ShapeDtypeStruct((8 * rows, step), BF)),
            grid=(1,),
            in_specs=[pl.BlockSpec((16 * rows, units), lambda i: (0, 0)), pl.BlockSpec((units, step), functools.partial(lambda c, i: (0, c), first // step))],
            out_specs=(pl.BlockSpec((8 * rows, step), lambda i: (0, 0)),) * 2,
            compiler_params=pltpu.CompilerParams(vmem_limit_bytes=20 * 2**20),
            name="down",
        )(hidden, down_weight)
        owns.append(own)
        recvs.append(flip(other, "dp", 2, 1))
        first += step
    kinds = [F32, F32, F32, BF, F32, BF, BF, BF]
    own0, own1, own2, own3, far0, far1, far2, far3 = pl.pallas_call(
        functools.partial(pair_kernel, len(SPLIT)),
        out_shape=[jax.ShapeDtypeStruct((rows, width), kind) for kind in kinds],
        in_specs=vmem_specs(2 * len(SPLIT)),
        out_specs=vmem_specs(8),
        compiler_params=pltpu.CompilerParams(vmem_limit_bytes=16 * 2**20),
        name="pair",
    )(*owns, *recvs)

    def send(x, mask):
        return flip(x.astype(BF), "tensor", 8, mask).astype(F32)

    sum2 = own2 + send(far2, 1) + send(own3, 2)
    sum0 = far0 + send(far3, 6)
    sum1 = own1 + send(far1, 1)
    total = own0 + send(sum2, 4) + send(sum0, 1) + send(sum1, 2)
    return (tokens.astype(F32) + total).astype(BF)


def generic_device(tokens, norm_gain, gate_weight, up_weight, down_weight):
    normed = scaled(tokens, inverse_rms(tokens), norm_gain)
    gathered = lax.all_gather(normed, ("dp", "tensor"), axis=0, tiled=True)
    gate_out = jnp.dot(gathered, gate_weight, preferred_element_type=F32)
    up_out = jnp.dot(gathered, up_weight, preferred_element_type=F32)
    hidden = (jax.nn.silu(gate_out) * up_out).astype(BF)
    partial = jnp.dot(hidden, down_weight, preferred_element_type=F32)
    summed = lax.psum_scatter(partial, ("dp", "tensor"), scatter_dimension=0, tiled=True)
    return (tokens.astype(F32) + summed).astype(BF)


def solution(mesh):
    tuned = mesh.shape["dp"] == 2 and mesh.shape["tensor"] == 8
    in_specs = (
        P(("groups", "dp", "tensor"), None),
        P(),
        P(None, ("dp", "tensor")),
        P(None, ("dp", "tensor")),
        P(("dp", "tensor"), None),
    )
    out_specs = P(("groups", "dp", "tensor"), None)
    return jax.shard_map(
        per_device if tuned else generic_device, mesh=mesh, in_specs=in_specs, out_specs=out_specs, check_vma=False
    )
```

```python
import functools

import jax
import jax.numpy as jnp
from jax import lax
from jax.experimental import pallas as pl
from jax.experimental.pallas import tpu as pltpu
from jax.sharding import PartitionSpec as P

BF = jnp.bfloat16
F32 = jnp.float32
SPLIT = (3, 1)
COST = 4
FETCHES = (2, 4)
CHUNK = 1024
ORDER = (0, 2, 3, 6, 1, 5, 7, 4)


def flip(x, axis, size, mask):
    return lax.ppermute(x, axis, [(i, i ^ mask) for i in range(size)])


def inverse_rms(rows):
    widened = rows.astype(F32)
    return lax.rsqrt(jnp.mean(widened * widened, axis=-1, keepdims=True) + 1e-05)


def scaled(rows, inv_rms, gain):
    return (rows.astype(F32) * inv_rms * gain).astype(BF)


def vmem_specs(count):
    return [pl.BlockSpec(memory_space=pltpu.VMEM)] * count


def fetch_kernel(first, after, *refs):
    gate, up = refs[:2]
    gate_out, up_out, mark, sems = refs[2 + after :]
    depth = gate_out.shape[0]
    copies = [
        pltpu.make_async_copy(src.at[pl.ds(first, depth)], dst, sems.at[i])
        for i, (src, dst) in enumerate([(gate, gate_out), (up, up_out)])
    ]
    for copy in copies:
        copy.start()
    mark[...] = jnp.zeros_like(mark)
    for copy in copies:
        copy.wait()


def fetch(gate, up, first, depth, shape, after):
    units = gate.shape[1]
    return pl.pallas_call(
        functools.partial(fetch_kernel, first, len(after)),
        out_shape=[pltpu.VMEM((depth, units), BF)] * 2 + [pltpu.VMEM(shape, BF)],
        in_specs=[pl.BlockSpec(memory_space=pltpu.HBM)] * 2 + [pl.BlockSpec(memory_space=pl.ANY)] * len(after),
        out_specs=vmem_specs(3),
        scratch_shapes=[pltpu.SemaphoreType.DMA((2,))],
        compiler_params=pltpu.CompilerParams(vmem_limit_bytes=1 * 2**20),
        cost_estimate=pl.CostEstimate(flops=0, bytes_accessed=COST * depth * units, transcendentals=0),
        name=f"fetch_{first}",
    )(hbm(gate), hbm(up), *after)


def hidden_kernel(held, *refs):
    near, (far_last, gain), rest = refs[:12], refs[12:14], refs[14:]
    pieces = list(near) + [far_last.at[8 * i : 8 * i + 8] for i in range(4)]
    pieces = [pieces[i] for i in ORDER + tuple(8 + i for i in ORDER)]
    gates, ups, (gate, up, out, gate_late, up_late, sems) = rest[:held], rest[held : 2 * held], rest[2 * held :]
    late, depth = gate_late.shape[:2]
    base = gate.shape[0] - late * depth
    copies = []
    for k in range(late):
        for i, (src, dst) in enumerate([(gate, gate_late), (up, up_late)]):
            copies.append(pltpu.make_async_copy(src.at[pl.ds(base + k * depth, depth)], dst.at[k], sems.at[k, i]))
            copies[-1].start()
    inv_rms = [inverse_rms(p[...]) for p in pieces]
    gate_out = up_out = 0.0
    first = 0
    for k in range(held + late):
        size = gates[k].shape[0] if k < held else depth
        cols = slice(first, first + size)
        rows = jnp.concatenate([scaled(p[:, cols], inv, gain[:, cols]) for p, inv in zip(pieces, inv_rms)], axis=0)
        if k >= held:
            copies[2 * (k - held)].wait()
            copies[2 * (k - held) + 1].wait()
        gate_block = gates[k][...] if k < held else gate_late[k - held]
        up_block = ups[k][...] if k < held else up_late[k - held]
        gate_out += jnp.dot(rows, gate_block, preferred_element_type=F32)
        up_out += jnp.dot(rows, up_block, preferred_element_type=F32)
        first += size
    out[...] = (jax.nn.silu(gate_out) * up_out).astype(BF)


def down_kernel(hidden, down, own, other):
    half = own.shape[0]
    part = jnp.dot(hidden[...], down[...], preferred_element_type=F32)
    own[...] = part[:half]
    other[...] = part[half:].astype(BF)


def pair_kernel(chunks, *refs):
    owns, recvs, outs = refs[:chunks], refs[chunks : 2 * chunks], refs[2 * chunks :]
    rows = outs[0].shape[0]
    first = 0
    for c in range(chunks):
        step = owns[c].shape[1]
        total = owns[c][...] + recvs[c][...].astype(F32)
        for d, out in enumerate(outs):
            out[:, first : first + step] = total[d * rows : (d + 1) * rows].astype(out.dtype)
        first += step


def sums_kernel(own2, far2, own3, own1, far1, sum2, sum1):
    sum2[...] = (own2[...] + far2[...].astype(F32) + own3[...].astype(F32)).astype(BF)
    sum1[...] = (own1[...] + far1[...].astype(F32)).astype(BF)


def hbm(x):
    return pltpu.with_memory_space_constraint(x, pltpu.HBM)


def join_kernel(*refs):
    pieces, out = refs[:-2], refs[-1]
    out[...] = jnp.concatenate([p[...] for p in pieces], axis=0)


def join_after(pieces, mark):
    rows = sum(p.shape[0] for p in pieces)
    return pl.pallas_call(
        join_kernel,
        out_shape=pltpu.VMEM((rows, pieces[0].shape[1]), BF),
        in_specs=vmem_specs(len(pieces)) + [pl.BlockSpec(memory_space=pl.ANY)],
        out_specs=vmem_specs(1)[0],
        compiler_params=pltpu.CompilerParams(vmem_limit_bytes=2 * 2**20),
        name="join",
    )(*pieces, mark)


def tie(x, mark):
    return x + mark


def pin(x):
    return pltpu.with_memory_space_constraint(x, pltpu.VMEM)


def per_device(tokens, norm_gain, gate_weight, up_weight, down_weight):
    rows, width = tokens.shape
    units = gate_weight.shape[1]
    def hop(x, mask):
        return flip(x, "tensor", 8, mask)

    sizes = [CHUNK * n for n in FETCHES]
    at1, at2, at4 = hop(tokens, 1), hop(tokens, 2), hop(tokens, 4)
    early = fetch(gate_weight, up_weight, 0, sizes[0], tokens.shape, [])
    at4t = tie(at4, early[2])
    at7, at3 = hop(tie(at1, early[2]), 6), hop(tie(at2, early[2]), 1)
    at6, at5 = hop(at4t, 2), hop(at4t, 1)
    later = fetch(gate_weight, up_weight, sizes[0], sizes[1], tokens.shape, [at4])
    mine = [tokens, at1, at2, at4]
    last = [at7, at3, at6, at5]
    far_mine = [flip(p, "dp", 2, 1) for p in mine]
    far_last = flip(join_after(last, later[2]), "dp", 2, 1)
    held = [early, later]
    pieces = mine + last + far_mine + [far_last]
    late = ((width - sum(sizes)) // CHUNK, CHUNK, units)
    hidden = pl.pallas_call(
        functools.partial(hidden_kernel, len(held)),
        out_shape=jax.ShapeDtypeStruct((16 * rows, units), BF),
        in_specs=vmem_specs(14 + 2 * len(held)) + [pl.BlockSpec(memory_space=pltpu.HBM)] * 2,
        out_specs=vmem_specs(1)[0],
        scratch_shapes=[pltpu.VMEM(late, BF), pltpu.VMEM(late, BF), pltpu.SemaphoreType.DMA((late[0], 2))],
        compiler_params=pltpu.CompilerParams(vmem_limit_bytes=24 * 2**20),
        name="hidden",
    )(*pieces, norm_gain.reshape(1, width), *[pin(f[0]) for f in held], *[pin(f[1]) for f in held], hbm(gate_weight), hbm(up_weight))
    first, unit = 0, width // sum(SPLIT)
    owns, recvs = [], []
    for share in SPLIT:
        step = share * unit
        own, other = pl.pallas_call(
            down_kernel,
            out_shape=(jax.ShapeDtypeStruct((8 * rows, step), F32), jax.ShapeDtypeStruct((8 * rows, step), BF)),
            grid=(1,),
            in_specs=[pl.BlockSpec((16 * rows, units), lambda i: (0, 0)), pl.BlockSpec((units, step), functools.partial(lambda c, i: (0, c), first // step))],
            out_specs=(pl.BlockSpec((8 * rows, step), lambda i: (0, 0)),) * 2,
            compiler_params=pltpu.CompilerParams(vmem_limit_bytes=20 * 2**20),
            name="down",
        )(hidden, down_weight)
        owns.append(own)
        recvs.append(flip(other, "dp", 2, 1))
        first += step
    kinds = [F32, F32, F32, BF, F32, BF, BF, BF]
    own0, own1, own2, own3, far0, far1, far2, far3 = pl.pallas_call(
        functools.partial(pair_kernel, len(SPLIT)),
        out_shape=[jax.ShapeDtypeStruct((rows, width), kind) for kind in kinds],
        in_specs=vmem_specs(2 * len(SPLIT)),
        out_specs=vmem_specs(8),
        compiler_params=pltpu.CompilerParams(vmem_limit_bytes=16 * 2**20),
        name="pair",
    )(*owns, *recvs)

    def send(x, mask):
        return flip(x.astype(BF), "tensor", 8, mask).astype(F32)

    sum2, sum1 = pl.pallas_call(
        sums_kernel,
        out_shape=[pltpu.VMEM((rows, width), BF)] * 2,
        in_specs=vmem_specs(5),
        out_specs=vmem_specs(2),
        compiler_params=pltpu.CompilerParams(vmem_limit_bytes=4 * 2**20),
        name="sums",
    )(own2, hop(far2, 1), hop(own3, 2), own1, hop(far1, 1))
    sum0 = far0 + send(far3, 6)
    total = own0 + send(sum2, 4) + send(sum1, 2) + send(sum0, 1)
    return (tokens.astype(F32) + total).astype(BF)


def generic_device(tokens, norm_gain, gate_weight, up_weight, down_weight):
    normed = scaled(tokens, inverse_rms(tokens), norm_gain)
    gathered = lax.all_gather(normed, ("dp", "tensor"), axis=0, tiled=True)
    gate_out = jnp.dot(gathered, gate_weight, preferred_element_type=F32)
    up_out = jnp.dot(gathered, up_weight, preferred_element_type=F32)
    hidden = (jax.nn.silu(gate_out) * up_out).astype(BF)
    partial = jnp.dot(hidden, down_weight, preferred_element_type=F32)
    summed = lax.psum_scatter(partial, ("dp", "tensor"), scatter_dimension=0, tiled=True)
    return (tokens.astype(F32) + summed).astype(BF)


def solution(mesh):
    tuned = mesh.shape["dp"] == 2 and mesh.shape["tensor"] == 8
    in_specs = (
        P(("groups", "dp", "tensor"), None),
        P(),
        P(None, ("dp", "tensor")),
        P(None, ("dp", "tensor")),
        P(("dp", "tensor"), None),
    )
    out_specs = P(("groups", "dp", "tensor"), None)
    return jax.shard_map(
        per_device if tuned else generic_device, mesh=mesh, in_specs=in_specs, out_specs=out_specs, check_vma=False
    )
```

```python
import functools

import jax
import jax.numpy as jnp
from jax import lax
from jax.experimental import pallas as pl
from jax.experimental.pallas import tpu as pltpu
from jax.sharding import PartitionSpec as P

BF = jnp.bfloat16
F32 = jnp.float32
SPLIT = (3, 1)
COST = 4
FETCHES = (5, 8)
CHUNK = 512
ORDER = (0, 2, 3, 6, 1, 5, 7, 4)


def flip(x, axis, size, mask):
    return lax.ppermute(x, axis, [(i, i ^ mask) for i in range(size)])


def inverse_rms(rows):
    widened = rows.astype(F32)
    return lax.rsqrt(jnp.mean(widened * widened, axis=-1, keepdims=True) + 1e-05)


def scaled(rows, inv_rms, gain):
    return (rows.astype(F32) * inv_rms * gain).astype(BF)


def vmem_specs(count):
    return [pl.BlockSpec(memory_space=pltpu.VMEM)] * count


def fetch_kernel(first, after, *refs):
    gate, up = refs[:2]
    gate_out, up_out, mark, sems = refs[2 + after :]
    depth = gate_out.shape[0]
    copies = [
        pltpu.make_async_copy(src.at[pl.ds(first, depth)], dst, sems.at[i])
        for i, (src, dst) in enumerate([(gate, gate_out), (up, up_out)])
    ]
    for copy in copies:
        copy.start()
    mark[...] = jnp.zeros_like(mark)
    for copy in copies:
        copy.wait()


def fetch(gate, up, first, depth, shape, after):
    units = gate.shape[1]
    return pl.pallas_call(
        functools.partial(fetch_kernel, first, len(after)),
        out_shape=[pltpu.VMEM((depth, units), BF)] * 2 + [pltpu.VMEM(shape, BF)],
        in_specs=[pl.BlockSpec(memory_space=pltpu.HBM)] * 2 + [pl.BlockSpec(memory_space=pl.ANY)] * len(after),
        out_specs=vmem_specs(3),
        scratch_shapes=[pltpu.SemaphoreType.DMA((2,))],
        compiler_params=pltpu.CompilerParams(vmem_limit_bytes=1 * 2**20),
        cost_estimate=pl.CostEstimate(flops=0, bytes_accessed=COST * depth * units, transcendentals=0),
        name=f"fetch_{first}",
    )(hbm(gate), hbm(up), *after)


def hidden_kernel(held, *refs):
    near, (far_last, gain), rest = refs[:12], refs[12:14], refs[14:]
    pieces = list(near) + [far_last.at[8 * i : 8 * i + 8] for i in range(4)]
    pieces = [pieces[i] for i in ORDER + tuple(8 + i for i in ORDER)]
    gates, ups, (gate, up, out, gate_late, up_late, sems) = rest[:held], rest[held : 2 * held], rest[2 * held :]
    late, depth = gate_late.shape[:2]
    base = gate.shape[0] - late * depth
    copies = []
    for k in range(late):
        for i, (src, dst) in enumerate([(gate, gate_late), (up, up_late)]):
            copies.append(pltpu.make_async_copy(src.at[pl.ds(base + k * depth, depth)], dst.at[k], sems.at[k, i]))
            copies[-1].start()
    inv_rms = [inverse_rms(p[...]) for p in pieces]
    gate_out = up_out = 0.0
    first = 0
    for k in range(held + late):
        size = gates[k].shape[0] if k < held else depth
        cols = slice(first, first + size)
        rows = jnp.concatenate([scaled(p[:, cols], inv, gain[:, cols]) for p, inv in zip(pieces, inv_rms)], axis=0)
        if k >= held:
            copies[2 * (k - held)].wait()
            copies[2 * (k - held) + 1].wait()
        gate_block = gates[k][...] if k < held else gate_late[k - held]
        up_block = ups[k][...] if k < held else up_late[k - held]
        gate_out += jnp.dot(rows, gate_block, preferred_element_type=F32)
        up_out += jnp.dot(rows, up_block, preferred_element_type=F32)
        first += size
    out[...] = (jax.nn.silu(gate_out) * up_out).astype(BF)


def down_kernel(hidden, down, own, other):
    half = own.shape[0]
    part = jnp.dot(hidden[...], down[...], preferred_element_type=F32)
    own[...] = part[:half]
    other[...] = part[half:].astype(BF)


def pair_kernel(chunks, *refs):
    owns, recvs, outs = refs[:chunks], refs[chunks : 2 * chunks], refs[2 * chunks :]
    rows = outs[0].shape[0]
    first = 0
    for c in range(chunks):
        step = owns[c].shape[1]
        total = owns[c][...] + recvs[c][...].astype(F32)
        for d, out in enumerate(outs):
            out[:, first : first + step] = total[d * rows : (d + 1) * rows].astype(out.dtype)
        first += step


def sums_kernel(own2, far2, own3, own1, far1, sum2, sum1):
    sum2[...] = (own2[...] + far2[...].astype(F32) + own3[...].astype(F32)).astype(BF)
    sum1[...] = (own1[...] + far1[...].astype(F32)).astype(BF)


def hbm(x):
    return pltpu.with_memory_space_constraint(x, pltpu.HBM)


def join_kernel(*refs):
    pieces, out = refs[:-2], refs[-1]
    out[...] = jnp.concatenate([p[...] for p in pieces], axis=0)


def join_after(pieces, mark):
    rows = sum(p.shape[0] for p in pieces)
    return pl.pallas_call(
        join_kernel,
        out_shape=pltpu.VMEM((rows, pieces[0].shape[1]), BF),
        in_specs=vmem_specs(len(pieces)) + [pl.BlockSpec(memory_space=pl.ANY)],
        out_specs=vmem_specs(1)[0],
        compiler_params=pltpu.CompilerParams(vmem_limit_bytes=2 * 2**20),
        name="join",
    )(*pieces, mark)


def tie(x, mark):
    return x + mark


def pin(x):
    return pltpu.with_memory_space_constraint(x, pltpu.VMEM)


def per_device(tokens, norm_gain, gate_weight, up_weight, down_weight):
    rows, width = tokens.shape
    units = gate_weight.shape[1]
    def hop(x, mask):
        return flip(x, "tensor", 8, mask)

    sizes = [CHUNK * n for n in FETCHES]
    at1, at2, at4 = hop(tokens, 1), hop(tokens, 2), hop(tokens, 4)
    early = fetch(gate_weight, up_weight, 0, sizes[0], tokens.shape, [])
    at4t = tie(at4, early[2])
    at7, at3 = hop(tie(at1, early[2]), 6), hop(tie(at2, early[2]), 1)
    at6, at5 = hop(at4t, 2), hop(at4t, 1)
    later = fetch(gate_weight, up_weight, sizes[0], sizes[1], tokens.shape, [at4])
    mine = [tokens, at1, at2, at4]
    last = [at7, at3, at6, at5]
    far_mine = [flip(p, "dp", 2, 1) for p in mine]
    far_last = flip(join_after(last, later[2]), "dp", 2, 1)
    held = [early, later]
    pieces = mine + last + far_mine + [far_last]
    late = ((width - sum(sizes)) // CHUNK, CHUNK, units)
    hidden = pl.pallas_call(
        functools.partial(hidden_kernel, len(held)),
        out_shape=jax.ShapeDtypeStruct((16 * rows, units), BF),
        in_specs=vmem_specs(14 + 2 * len(held)) + [pl.BlockSpec(memory_space=pltpu.HBM)] * 2,
        out_specs=vmem_specs(1)[0],
        scratch_shapes=[pltpu.VMEM(late, BF), pltpu.VMEM(late, BF), pltpu.SemaphoreType.DMA((late[0], 2))],
        compiler_params=pltpu.CompilerParams(vmem_limit_bytes=24 * 2**20),
        name="hidden",
    )(*pieces, norm_gain.reshape(1, width), *[pin(f[0]) for f in held], *[pin(f[1]) for f in held], hbm(gate_weight), hbm(up_weight))
    first, unit = 0, width // sum(SPLIT)
    owns, recvs = [], []
    for share in SPLIT:
        step = share * unit
        own, other = pl.pallas_call(
            down_kernel,
            out_shape=(jax.ShapeDtypeStruct((8 * rows, step), F32), jax.ShapeDtypeStruct((8 * rows, step), BF)),
            grid=(1,),
            in_specs=[pl.BlockSpec((16 * rows, units), lambda i: (0, 0)), pl.BlockSpec((units, step), functools.partial(lambda c, i: (0, c), first // step))],
            out_specs=(pl.BlockSpec((8 * rows, step), lambda i: (0, 0)),) * 2,
            compiler_params=pltpu.CompilerParams(vmem_limit_bytes=20 * 2**20),
            name="down",
        )(hidden, down_weight)
        owns.append(own)
        recvs.append(flip(other, "dp", 2, 1))
        first += step
    kinds = [F32, F32, F32, BF, F32, BF, BF, BF]
    own0, own1, own2, own3, far0, far1, far2, far3 = pl.pallas_call(
        functools.partial(pair_kernel, len(SPLIT)),
        out_shape=[jax.ShapeDtypeStruct((rows, width), kind) for kind in kinds],
        in_specs=vmem_specs(2 * len(SPLIT)),
        out_specs=vmem_specs(8),
        compiler_params=pltpu.CompilerParams(vmem_limit_bytes=16 * 2**20),
        name="pair",
    )(*owns, *recvs)

    def send(x, mask):
        return flip(x.astype(BF), "tensor", 8, mask).astype(F32)

    sum2, sum1 = pl.pallas_call(
        sums_kernel,
        out_shape=[pltpu.VMEM((rows, width), BF)] * 2,
        in_specs=vmem_specs(5),
        out_specs=vmem_specs(2),
        compiler_params=pltpu.CompilerParams(vmem_limit_bytes=4 * 2**20),
        name="sums",
    )(own2, hop(far2, 1), hop(own3, 2), own1, hop(far1, 1))
    sum0 = far0 + send(far3, 6)
    total = own0 + send(sum2, 4) + send(sum1, 2) + send(sum0, 1)
    return (tokens.astype(F32) + total).astype(BF)


def generic_device(tokens, norm_gain, gate_weight, up_weight, down_weight):
    normed = scaled(tokens, inverse_rms(tokens), norm_gain)
    gathered = lax.all_gather(normed, ("dp", "tensor"), axis=0, tiled=True)
    gate_out = jnp.dot(gathered, gate_weight, preferred_element_type=F32)
    up_out = jnp.dot(gathered, up_weight, preferred_element_type=F32)
    hidden = (jax.nn.silu(gate_out) * up_out).astype(BF)
    partial = jnp.dot(hidden, down_weight, preferred_element_type=F32)
    summed = lax.psum_scatter(partial, ("dp", "tensor"), scatter_dimension=0, tiled=True)
    return (tokens.astype(F32) + summed).astype(BF)


def solution(mesh):
    tuned = mesh.shape["dp"] == 2 and mesh.shape["tensor"] == 8
    in_specs = (
        P(("groups", "dp", "tensor"), None),
        P(),
        P(None, ("dp", "tensor")),
        P(None, ("dp", "tensor")),
        P(("dp", "tensor"), None),
    )
    out_specs = P(("groups", "dp", "tensor"), None)
    return jax.shard_map(
        per_device if tuned else generic_device, mesh=mesh, in_specs=in_specs, out_specs=out_specs, check_vma=False
    )
```
